32 devices in a mesh: groups: 2 (over y), dp: 2 (over core), chan: 8 (over z, x).
Axes of the slice: x: 2, y: 2, z: 4, core: 2. Of those that a mesh axis runs over, the one named last changes fastest.
Arguments:
- counts: int32 [4], P('groups'), parts along dimension 0, may hold values from 0 to 2, as said below
- inputs: bfloat16 [8, 1024, 8192], P(('groups', 'dp'), None, 'chan'), parts along dimension 0, may hold values from -6 to 6
- cotangent: bfloat16 [8, 1024, 8192], P(('groups', 'dp'), None, 'chan'), parts along dimension 0, may hold values from -6 to 6
- basis: float32 [128, 128], replicated, may hold values from -0.5 to 0.5
- eigvals: float32 [8192, 128], P('chan'), may hold values from 0.05 to 150
- query_context: bfloat16 [1024, 8192], P(None, 'chan'), may hold values from -6 to 6
- query_cotangent: bfloat16 [64, 8192], P(None, 'chan'), may hold values from -6 to 6
- query_pos: int32 [64], replicated, may hold values from 127 to 1023
Outputs:
- scores: float32 [8, 64], P(('groups', 'dp')), parts along dimension 0
The draws below stay inside these ranges and needn't reach their ends.
There are 2 independent parts, one for each index of `groups`. The reference program is written for one: setup_inputs(seed, part) draws one part's arguments, and reference() takes and returns one part's arrays. A program takes and returns all parts, laid end to end along the dimension named above; an argument that names none is the same for every part. Nothing has to cross between parts.
Inputs may be any that keep to these rules, and one draw needn't show every extreme that they name: One of the two counts is 2, the other at most 1.
All inputs are finite; a program needn't handle non-finite values.
Results may differ from the reference program's by a relative error of at most 0.0003.
Values may be sent and summed in bfloat16 or wider, within the bound.
No kernel may reach another device: no remote copies, remote signals or barrier semaphores. Data moves between devices by JAX's collectives and lax.ppermute only.
A program may use at most 576 MiB of HBM per device.

```python
import math
import jax
import jax.numpy as jnp
from jax import lax

D = 8192
K = 128
L = 1024
CAP = 2
Q = 64
LQ = 1024
SLOTS = 4
N_DP = 2


def draw_counts(key, part):
    key = jax.random.fold_in(key, 3)
    first_key, second_key = jax.random.split(key)
    busy_index = jax.random.randint(first_key, (), 0, N_DP)
    light_count = jax.random.randint(second_key, (), 0, CAP // 2 + 1)
    return jnp.where(jnp.arange(N_DP) == busy_index, CAP, light_count).astype(jnp.int32)


def draw_eigvals(key, part):
    key = jax.random.fold_in(key, 7)
    first_key = jax.random.fold_in(key, 0)
    base_vals = jnp.exp(jax.random.uniform(first_key, (D, K), jnp.float32, math.log(0.05), math.log(5.0)))
    trend = jnp.exp(math.log(3.0) * jnp.arange(D, dtype=jnp.float32) / D)[:, None]
    return (base_vals * trend).astype(jnp.float32)


def with_ends(drawn, rng, low, top_value):
    longest = drawn.shape.index(max(drawn.shape))
    spots = []
    for shift in (0, 1):
        where = [jax.random.randint(jax.random.fold_in(rng, axis), (), 0, length) for axis, length in enumerate(drawn.shape)]
        where[longest] = (where[longest] + shift) % drawn.shape[longest]
        spots.append(tuple(where))
    return drawn.at[spots[0]].set(low).at[spots[1]].set(top_value)


def block_scale(own_key, dims, shards, least, largest):
    loudness = 1.0
    for dim, blocks in shards:
        heights = jax.random.uniform(jax.random.fold_in(jax.random.fold_in(own_key, 6), dim), (blocks,), jnp.float32, least / len(shards), largest / len(shards))
        loudness = loudness * jnp.repeat(jnp.exp(heights), dims[dim] // blocks).reshape((-1,) + (1,) * (len(dims) - 1 - dim))
    return loudness


def scatter_about(stream_key, dims, scale, limit, cuts=(), kind=jnp.bfloat16):
    entries = jax.random.normal(stream_key, dims, jnp.float32) * scale
    if len(cuts) > 0:
        entries = block_scale(stream_key, dims, cuts, -0.22, 0.18) * entries
    return jnp.clip(entries, min=-limit, max=limit).astype(kind)


def setup_inputs(seed: int = 0, part: int = 0) -> dict:
    streams_of = jax.random.split(jax.random.key(seed), 9)
    part_keys = jax.random.split(jax.random.fold_in(streams_of[8], part), 9)
    return {
        "counts": draw_counts(jax.random.fold_in(jax.random.fold_in(streams_of[8], part), 71), part),
        "inputs": scatter_about(part_keys[1], (SLOTS, L, D), 1.0, 6.0, ((0, 2), (2, 8))),
        "cotangent": scatter_about(part_keys[2], (SLOTS, L, D), 1.0, 6.0, ((0, 2), (2, 8))),
        "basis": scatter_about(streams_of[3], (K, K), K ** -0.5, 0.5, (), jnp.float32),
        "eigvals": draw_eigvals(jax.random.fold_in(streams_of[8], 71), part),
        "query_context": scatter_about(streams_of[5], (LQ, D), 1.0, 6.0, ((1, 8),)),
        "query_cotangent": scatter_about(streams_of[6], (Q, D), 1.0, 6.0, ((1, 8),)),
        "query_pos": with_ends(jax.random.randint(streams_of[7], (Q,), K - 1, LQ), jax.random.fold_in(streams_of[7], 1), K - 1, LQ - 1).astype(jnp.int32),
    }


damping = 0.1

def tap_grads(window_in, window_ct):
    inputs_f = window_in.astype(jnp.float32)
    cotan_f = window_ct.astype(jnp.float32)
    padded = jnp.concatenate([jnp.zeros((K, D), jnp.float32), inputs_f], 0)

    def lag_sum(lag):
        shifted = lax.dynamic_slice_in_dim(padded, (K - lag).astype(jnp.int32), L, 0)
        return lax.optimization_barrier(jnp.sum(cotan_f * shifted, axis=0))
    return lax.map(lag_sum, jnp.arange(K, dtype=jnp.int32)).T

def reference(counts, inputs, cotangent, basis, eigvals, query_context, query_cotangent, query_pos):
    slot_grads = lax.map(lambda pair: tap_grads(pair[0], pair[1]), (inputs, cotangent))
    rotated = jnp.einsum('sck,ka->sca', slot_grads, basis, precision=lax.Precision.HIGHEST)
    row_index = (query_pos[:, None] - jnp.arange(K, dtype=jnp.int32)[None, :]).astype(jnp.int32)
    context_rows = query_context.astype(jnp.float32)[row_index]
    query_grad = context_rows * query_cotangent.astype(jnp.float32)[:, None, :]
    query_rot = jnp.einsum('qkc,ka->qca', query_grad, basis, precision=lax.Precision.HIGHEST)
    weight = 1.0 / (eigvals + damping)
    self_norm = jnp.einsum('sca,ca->s', rotated * rotated, weight, precision=lax.Precision.HIGHEST)
    raw_scores = jnp.einsum('sca,qca->sq', rotated * weight[None], query_rot, precision=lax.Precision.HIGHEST)
    slot_ids = jnp.arange(SLOTS, dtype=jnp.int32)
    live_rows = slot_ids % CAP < counts[slot_ids // CAP]
    safe_norm = jnp.where(live_rows, self_norm, jnp.float32(1.0))
    return jnp.where(live_rows[:, None], raw_scores / jnp.sqrt(safe_norm)[:, None], jnp.float32(0.0))
```

```python
import functools

import jax
import jax.numpy as jnp
import ml_dtypes
import numpy as np
from jax import lax
from jax.experimental import pallas as pl
from jax.experimental.pallas import tpu as pltpu
from jax.sharding import PartitionSpec as P

damping = 0.1
f32 = jnp.float32
bf16 = jnp.bfloat16


def transform_tables(taps):
    freq = np.arange(taps)
    angle = np.pi / taps * np.arange(taps)[:, None] * (freq + 0.5)[None, :]
    sign = np.where(freq % 2 == 0, 1.0, -1.0)
    real, imag = np.cos(angle), -np.sin(angle)
    forward = []
    for table in (np.concatenate([real, imag], 1), np.concatenate([sign * imag, -sign * real], 1)):
        high = table.astype(ml_dtypes.bfloat16)
        low = (table - high.astype(np.float64)).astype(ml_dtypes.bfloat16)
        forward.append(np.concatenate([high, low], 0))
    inverse = np.concatenate([np.sin(angle) * sign, np.cos(angle) * sign], 1).T / taps
    return np.stack(forward), inverse.astype(np.float32)


def split(value):
    high = value.astype(bf16)
    return high, (value - high.astype(f32)).astype(bf16)


def dot(a, b):
    return jnp.dot(a, b, preferred_element_type=f32)


def dot_nt(a, b):
    return lax.dot_general(a, b, (((1,), (1,)), ((), ())), preferred_element_type=f32)


def local_kernel(
    counts_hbm, pos_hbm, x_hbm, g_hbm, basis_hbm, eig_hbm, ctx_hbm, qct_hbm, fwd_hbm, inv_hbm, out_ref,
    xbuf, gbuf, ctxbuf, eigbuf, basisbuf, qctbuf, fwd, inv,
    x_turned, g_turned, rot_mat, back, vbuf, ctxf, qctf, raw, norm, counts_ref, pos_ref, sems, wsems,
):
    capacity, cb_count, length, cb = xbuf.shape
    taps = basisbuf.shape[0]
    queries = pos_ref.shape[0]
    blocks = length // taps
    tiles = cb // 128

    def columns(c):
        return pl.ds(c * cb, cb)

    scalars = [
        pltpu.make_async_copy(counts_hbm, counts_ref, sems.at[5 + cb_count]),
        pltpu.make_async_copy(pos_hbm, pos_ref, sems.at[6 + cb_count]),
    ]
    small = [
        pltpu.make_async_copy(fwd_hbm, fwd, sems.at[0]),
        pltpu.make_async_copy(basis_hbm, basisbuf, sems.at[1]),
        pltpu.make_async_copy(inv_hbm, inv, sems.at[2]),
        pltpu.make_async_copy(qct_hbm, qctbuf, sems.at[3]),
        pltpu.make_async_copy(eig_hbm, eigbuf, sems.at[4]),
    ]
    ctx_copies = [
        pltpu.make_async_copy(ctx_hbm.at[:, columns(c)], ctxbuf.at[c], sems.at[5 + c]) for c in range(cb_count)
    ]

    def window_copies(s, c):
        return (
            pltpu.make_async_copy(x_hbm.at[s, :, columns(c)], xbuf.at[s, c], wsems.at[0, s, c]),
            pltpu.make_async_copy(g_hbm.at[s, :, columns(c)], gbuf.at[s, c], wsems.at[1, s, c]),
        )

    for copy in scalars + small[:3]:
        copy.start()
    scalars[0].wait()
    count = counts_ref[lax.axis_index("dp")]
    for c in range(cb_count):
        for s in range(capacity):
            @pl.when(s < count)
            def _():
                for copy in window_copies(s, c):
                    copy.start()
            if c == 0 and s == 0:
                for copy in small[3:]:
                    copy.start()
        ctx_copies[c].start()

    raw[...] = jnp.zeros_like(raw)
    norm[...] = jnp.zeros_like(norm)
    for copy in small[:3]:
        copy.wait()

    base_hi, base_lo = split(basisbuf[...])
    inv_hi, inv_lo = split(inv[...])
    rot_hi, rot_lo = split(dot(inv_hi, base_hi) + (dot(inv_hi, base_lo) + dot(inv_lo, base_hi)))
    rot_mat[...] = jnp.concatenate([rot_hi, rot_lo], 1)
    row = lax.broadcasted_iota(jnp.int32, (taps, taps), 0)
    col = lax.broadcasted_iota(jnp.int32, (taps, taps), 1)
    flip = (row + col == taps - 1).astype(bf16)
    flip_hi = dot(flip, base_hi).astype(bf16)
    back[...] = jnp.concatenate([flip_hi, flip_hi, dot(flip, base_lo).astype(bf16)], 1)
    for copy in small[3:] + scalars[1:]:
        copy.wait()
    for t in range(cb_count * tiles):
        qctf[t] = qctbuf[:, t * 128:(t + 1) * 128].astype(f32)

    rows = 32

    def cross(first):
        def stack(parity):
            parts = []
            for b in range(blocks):
                turned = x_turned if b % 2 == parity else g_turned
                parts.append(turned[first:first + rows, b * taps:(b + 1) * taps])
            both = jnp.concatenate(parts, 0)
            return jnp.concatenate([both, both], 1)

        spectra = [dot(stack(0), fwd[0]), dot(stack(1), fwd[1])]

        def parts_of(array, b):
            block = spectra[b % 2 if array == 0 else 1 - b % 2][b * rows:(b + 1) * rows]
            return block[:, :taps], block[:, taps:]

        for b in range(blocks):
            x_re, x_im = parts_of(0, b)
            g_re, g_im = parts_of(1, b)
            if b == 0:
                t_re, t_im = -x_re, -x_im
            elif b % 2:
                t_re, t_im = prev_re + x_re, prev_im + x_im
            else:
                t_re, t_im = prev_re - x_re, prev_im - x_im
            add_re = g_re * t_re + g_im * t_im
            add_im = g_im * t_re - g_re * t_im
            sum_re = add_re if b == 0 else sum_re + add_re
            sum_im = add_im if b == 0 else sum_im + add_im
            prev_re, prev_im = x_re, x_im
        return jnp.concatenate([sum_re, sum_im], 1)

    def filters(s, c):
        x_turned[...] = xbuf[s, c].T
        g_turned[...] = gbuf[s, c].T
        high, low = split(jnp.concatenate([cross(first) for first in range(0, cb, rows)], 0))
        twice = dot(high, rot_mat[...])
        rotated = twice[:, :taps] + (twice[:, taps:] + dot(low, rot_mat[:, :taps]))
        scaled = rotated / (eigbuf[pl.ds(pl.multiple_of(c * cb, cb), cb), :] + damping)
        norm[s] += jnp.sum((scaled * rotated).reshape(cb // 8, 8, taps), 0)
        high, low = split(scaled)
        turned = dot_nt(back[:, :2 * taps], jnp.concatenate([high, low], 1)) + dot_nt(back[:, 2 * taps:], high)
        for t in range(tiles):
            vbuf[s, c * tiles + t] = turned[:, t * 128:(t + 1) * 128]

    for c in range(cb_count):
        for s in range(capacity):
            @pl.when(s < count)
            def _():
                for copy in window_copies(s, c):
                    copy.wait()
        ctx_copies[c].wait()

        def filter_step(s, unused):
            filters(s, c)
            return unused

        lax.fori_loop(0, count, filter_step, 0)

    per_iter = min(16, queries)

    def probes(windows):
        def tile_step(t, unused):
            c, part_of = t // tiles, t % tiles
            for k in range(tiles):
                @pl.when(part_of == k)
                def _():
                    ctxf[...] = ctxbuf[c, :, k * 128:(k + 1) * 128].astype(f32)

            def probe(i, unused):
                filt = [vbuf[s, t] for s in range(windows)]
                for u in range(per_iter):
                    q = i * per_iter + u
                    start = jnp.clip(pos_ref[q] - (taps - 1), 0, length - taps)
                    piece = ctxf[pl.ds(start, taps), :]
                    cotangent = qctf[t, pl.ds(q, 1), :]
                    for s in range(windows):
                        part = jnp.sum((piece * filt[s]).reshape(taps // 8, 8, 128), 0)
                        raw[s, q] += part * cotangent
                return unused

            lax.fori_loop(0, queries // per_iter, probe, 0)
            return unused

        lax.fori_loop(0, cb_count * tiles, tile_step, 0)

    for windows in range(1, capacity + 1):
        @pl.when(count == windows)
        def _():
            probes(windows)

    for s in range(capacity):
        per_query = jnp.sum(raw[s], 1)
        lane_one = (lax.broadcasted_iota(jnp.int32, (1, 128), 1) == 0).astype(f32)
        own = jnp.where(s < count, jnp.sum(norm[s], 0, keepdims=True), lane_one)
        table = jnp.concatenate([per_query, jnp.broadcast_to(own, (128 - queries, 128))], 0)
        out_ref[pl.ds(s, 1), :] = jnp.sum(table.T, 0, keepdims=True)


def local_sums(counts, inputs, cotangent, basis, eigvals, query_context, query_cotangent, query_pos):
    capacity, length, width = inputs.shape
    taps = basis.shape[0]
    queries = query_pos.shape[0]
    cb = min(256, width)
    cb_count, tiles = width // cb, cb // 128
    forward, inverse = transform_tables(taps)
    hbm = pl.BlockSpec(memory_space=pl.ANY)
    return pl.pallas_call(
        local_kernel,
        out_shape=jax.ShapeDtypeStruct((capacity, 128), f32),
        in_specs=[hbm] * 10,
        out_specs=pl.BlockSpec(memory_space=pltpu.VMEM),
        scratch_shapes=[
            pltpu.VMEM((capacity, cb_count, length, cb), bf16),
            pltpu.VMEM((capacity, cb_count, length, cb), bf16),
            pltpu.VMEM((cb_count, length, cb), bf16),
            pltpu.VMEM((width, taps), f32),
            pltpu.VMEM((taps, taps), f32),
            pltpu.VMEM((queries, width), bf16),
            pltpu.VMEM((2, 2 * taps, 2 * taps), bf16),
            pltpu.VMEM((2 * taps, taps), f32),
            pltpu.VMEM((cb, length), bf16),
            pltpu.VMEM((cb, length), bf16),
            pltpu.VMEM((2 * taps, 2 * taps), bf16),
            pltpu.VMEM((taps, 3 * taps), bf16),
            pltpu.VMEM((capacity, cb_count * tiles, taps, 128), f32),
            pltpu.VMEM((length, 128), f32),
            pltpu.VMEM((cb_count * tiles, queries, 128), f32),
            pltpu.VMEM((capacity, queries, 8, 128), f32),
            pltpu.VMEM((capacity, 8, 128), f32),
            pltpu.SMEM(counts.shape, jnp.int32),
            pltpu.SMEM((queries,), jnp.int32),
            pltpu.SemaphoreType.DMA((7 + cb_count,)),
            pltpu.SemaphoreType.DMA((2, capacity, cb_count)),
        ],
        compiler_params=pltpu.CompilerParams(vmem_limit_bytes=62 * 1024 * 1024),
        cost_estimate=pl.CostEstimate(flops=4 * 10**9, bytes_accessed=11 * 2**20, transcendentals=0),
    )(
        counts, query_pos, inputs, cotangent, basis, eigvals, query_context, query_cotangent,
        jnp.asarray(forward), jnp.asarray(inverse),
    )


def sum_over(value, axis):
    size = lax.axis_size(axis)
    mask = 1
    while mask < size:
        value = value + lax.ppermute(value, axis, [(i, i ^ mask) for i in range(size)])
        mask *= 2
    return value


def body(counts, inputs, cotangent, basis, eigvals, query_context, query_cotangent, query_pos):
    capacity = inputs.shape[0]
    queries = query_pos.shape[0]
    sums = local_sums(counts, inputs, cotangent, basis, eigvals, query_context, query_cotangent, query_pos)
    sums = sum_over(sums, "chan")
    return sums[:, :queries] / jnp.sqrt(sums[:, queries:queries + 1])


def solution(mesh):
    return jax.shard_map(
        body,
        mesh=mesh,
        in_specs=(
            P("groups"),
            P(("groups", "dp"), None, "chan"),
            P(("groups", "dp"), None, "chan"),
            P(),
            P("chan", None),
            P(None, "chan"),
            P(None, "chan"),
            P(),
        ),
        out_specs=P(("groups", "dp"), None),
        check_vma=False,
    )
```

```python
import functools

import jax
import jax.numpy as jnp
import ml_dtypes
import numpy as np
from jax import lax
from jax.experimental import pallas as pl
from jax.experimental.pallas import tpu as pltpu
from jax.sharding import PartitionSpec as P

damping = 0.1
f32 = jnp.float32
bf16 = jnp.bfloat16


def transform_tables(taps):
    freq = np.arange(taps)
    angle = np.pi / taps * np.arange(taps)[:, None] * (freq + 0.5)[None, :]
    sign = np.where(freq % 2 == 0, 1.0, -1.0)
    real, imag = np.cos(angle), -np.sin(angle)
    forward = []
    for table in (np.concatenate([real, imag], 1), np.concatenate([sign * imag, -sign * real], 1)):
        high = table.astype(ml_dtypes.bfloat16)
        low = (table - high.astype(np.float64)).astype(ml_dtypes.bfloat16)
        forward.append(np.concatenate([high, low], 0))
    inverse = np.concatenate([np.sin(angle) * sign, np.cos(angle) * sign], 1).T / taps
    return np.stack(forward), inverse.astype(np.float32)


def split(value):
    high = value.astype(bf16)
    return high, (value - high.astype(f32)).astype(bf16)


def dot(a, b):
    return jnp.dot(a, b, preferred_element_type=f32)


def dot_nt(a, b):
    return lax.dot_general(a, b, (((1,), (1,)), ((), ())), preferred_element_type=f32)


def local_kernel(
    counts_hbm, pos_hbm, x_hbm, g_hbm, basis_hbm, eig_hbm, ctx_hbm, qct_hbm, fwd_hbm, inv_hbm, out_ref,
    xbuf, gbuf, ctxbuf, eigbuf, basisbuf, qctbuf, fwd, inv,
    x_turned, g_turned, acc_hi, acc_lo, rot_mat, back, vbuf, ctxf, qctf, raw, norm, counts_ref, pos_ref, start_ref, sems, wsems,
):
    capacity, cb_count, length, cb = xbuf.shape
    taps = basisbuf.shape[0]
    queries = pos_ref.shape[0]
    blocks = length // taps
    tiles = cb // 128
    width = cb_count * cb

    def columns(c):
        return pl.ds(pl.multiple_of(c * cb, cb), cb)

    scalars = [
        pltpu.make_async_copy(counts_hbm, counts_ref, sems.at[5 + cb_count]),
        pltpu.make_async_copy(pos_hbm, pos_ref, sems.at[6 + cb_count]),
    ]
    small = [
        pltpu.make_async_copy(fwd_hbm, fwd, sems.at[0]),
        pltpu.make_async_copy(basis_hbm, basisbuf, sems.at[1]),
        pltpu.make_async_copy(inv_hbm, inv, sems.at[2]),
        pltpu.make_async_copy(qct_hbm, qctbuf, sems.at[3]),
        pltpu.make_async_copy(eig_hbm, eigbuf, sems.at[4]),
    ]

    def context_copy(c):
        return pltpu.make_async_copy(ctx_hbm.at[:, columns(c)], ctxbuf.at[c], sems.at[5 + c])

    def window_copies(s, c):
        return (
            pltpu.make_async_copy(x_hbm.at[s, :, columns(c)], xbuf.at[s, c], wsems.at[0, s, c]),
            pltpu.make_async_copy(g_hbm.at[s, :, columns(c)], gbuf.at[s, c], wsems.at[1, s, c]),
        )

    for copy in scalars + small[:3]:
        copy.start()
    for c in range(cb_count):
        for copy in window_copies(0, c):
            copy.start()
        if c == 0:
            for copy in small[3:]:
                copy.start()
        context_copy(c).start()
    scalars[0].wait()
    count = counts_ref[lax.axis_index("dp")]
    for s in range(1, capacity):
        @pl.when(s < count)
        def _():
            for c in range(cb_count):
                for copy in window_copies(s, c):
                    copy.start()

    raw[...] = jnp.zeros_like(raw)
    norm[...] = jnp.zeros_like(norm)
    scalars[1].wait()

    def starts(q, unused):
        start_ref[q] = jnp.clip(pos_ref[q] - (taps - 1), 0, length - taps)
        return unused

    lax.fori_loop(0, queries, starts, 0)
    for copy in small[:3]:
        copy.wait()

    base_hi, base_lo = split(basisbuf[...])
    inv_hi, inv_lo = split(inv[...])
    rot_hi, rot_lo = split(dot(inv_hi, base_hi) + (dot(inv_hi, base_lo) + dot(inv_lo, base_hi)))
    rot_mat[...] = jnp.concatenate([rot_hi, rot_lo], 1)
    row = lax.broadcasted_iota(jnp.int32, (taps, taps), 0)
    col = lax.broadcasted_iota(jnp.int32, (taps, taps), 1)
    flip = (row + col == taps - 1).astype(bf16)
    flip_hi = dot(flip, base_hi).astype(bf16)
    back[...] = jnp.concatenate([flip_hi, flip_hi, dot(flip, base_lo).astype(bf16)], 1)

    rows = 32

    def cross(first):
        def stack(parity):
            parts = []
            for b in range(blocks):
                turned = x_turned if b % 2 == parity else g_turned
                parts.append(turned[first:first + rows, b * taps:(b + 1) * taps])
            both = jnp.concatenate(parts, 0)
            return jnp.concatenate([both, both], 1)

        spectra = [dot(stack(0), fwd[0]), dot(stack(1), fwd[1])]

        def parts_of(array, b):
            block = spectra[b % 2 if array == 0 else 1 - b % 2][b * rows:(b + 1) * rows]
            return block[:, :taps], block[:, taps:]

        for b in range(blocks):
            x_re, x_im = parts_of(0, b)
            g_re, g_im = parts_of(1, b)
            if b == 0:
                t_re, t_im = -x_re, -x_im
            elif b % 2:
                t_re, t_im = prev_re + x_re, prev_im + x_im
            else:
                t_re, t_im = prev_re - x_re, prev_im - x_im
            add_re = g_re * t_re + g_im * t_im
            add_im = g_im * t_re - g_re * t_im
            sum_re = add_re if b == 0 else sum_re + add_re
            sum_im = add_im if b == 0 else sum_im + add_im
            prev_re, prev_im = x_re, x_im
        return jnp.concatenate([sum_re, sum_im], 1)

    def spectra(s, c):
        for copy in window_copies(s, c):
            copy.wait()
        for t in range(0, cb, 128):
            for turned, buf in ((x_turned, xbuf), (g_turned, gbuf)):
                turned[t:t + 128, :] = buf[s, c, :, t:t + 128].T
        for first in range(0, cb, rows):
            place = pl.ds(pl.multiple_of(c * cb + first, rows), rows)
            acc_hi[place, :], acc_lo[place, :] = split(cross(first))

    def filters(s):
        @pl.when(s == 0)
        def _():
            eigbuf[...] = 1.0 / (eigbuf[...] + damping)

        twice = dot(acc_hi[...], rot_mat[...])
        rotated = twice[:, :taps] + (twice[:, taps:] + dot(acc_lo[...], rot_mat[:, :taps]))
        scaled = rotated * eigbuf[...]
        norm[s] = jnp.sum((scaled * rotated).reshape(width // 8, 8, taps), 0)
        high, low = split(scaled)
        turned = dot_nt(back[:, :2 * taps], jnp.concatenate([high, low], 1)) + dot_nt(back[:, 2 * taps:], high)
        for t in range(width // 128):
            vbuf[s, t] = turned[:, t * 128:(t + 1) * 128]

    for copy in small[3:]:
        copy.wait()
    for t in range(cb_count * tiles):
        qctf[t] = qctbuf[:, t * 128:(t + 1) * 128].astype(f32)

    def window_step(s, unused):
        def block_step(c, unused):
            spectra(s, c)
            return unused

        lax.fori_loop(0, cb_count, block_step, 0)
        filters(s)
        return unused

    lax.fori_loop(0, count, window_step, 0)
    for c in range(cb_count):
        context_copy(c).wait()

    @pl.when(count == 0)
    def _():
        for c in range(cb_count):
            for copy in window_copies(0, c):
                copy.wait()

    halves = 2
    depth = taps // halves

    def probes(windows):
        def tile_step(t, unused):
            for k in range(tiles):
                @pl.when(t % tiles == k)
                def _():
                    ctxf[...] = ctxbuf[t // tiles, :, k * 128:(k + 1) * 128].astype(f32)

            for h in range(halves):
                filt = [vbuf[s, t, h * depth:(h + 1) * depth, :] for s in range(windows)]
                for q in range(queries):
                    piece = ctxf[pl.ds(start_ref[q] + h * depth, depth), :]
                    cotangent = qctf[t, q:q + 1, :]
                    for s in range(windows):
                        part = jnp.sum((piece * filt[s]).reshape(depth // 8, 8, 128), 0)
                        raw[s, q] += part * cotangent
            return unused

        lax.fori_loop(0, width // 128, tile_step, 0)

    for windows in range(1, capacity + 1):
        @pl.when(count == windows)
        def _():
            probes(windows)

    for s in range(capacity):
        per_query = jnp.sum(raw[s], 1)
        lane_one = (lax.broadcasted_iota(jnp.int32, (1, 128), 1) == 0).astype(f32)
        own = jnp.where(s < count, jnp.sum(norm[s], 0, keepdims=True), lane_one)
        table = jnp.concatenate([per_query, jnp.broadcast_to(own, (queries, 128))], 0)
        out_ref[pl.ds(s, 1), :] = jnp.sum(table.T, 0, keepdims=True)


def local_sums(counts, inputs, cotangent, basis, eigvals, query_context, query_cotangent, query_pos):
    capacity, length, width = inputs.shape
    taps = basis.shape[0]
    queries = query_pos.shape[0]
    cb = min(512, width)
    cb_count, tiles = width // cb, cb // 128
    forward, inverse = transform_tables(taps)
    hbm = pl.BlockSpec(memory_space=pl.ANY)
    return pl.pallas_call(
        local_kernel,
        out_shape=jax.ShapeDtypeStruct((capacity, 128), f32),
        in_specs=[hbm] * 10,
        out_specs=pl.BlockSpec(memory_space=pltpu.VMEM),
        scratch_shapes=[
            pltpu.VMEM((capacity, cb_count, length, cb), bf16),
            pltpu.VMEM((capacity, cb_count, length, cb), bf16),
            pltpu.VMEM((cb_count, length, cb), bf16),
            pltpu.VMEM((width, taps), f32),
            pltpu.VMEM((taps, taps), f32),
            pltpu.VMEM((queries, width), bf16),
            pltpu.VMEM((2, 2 * taps, 2 * taps), bf16),
            pltpu.VMEM((2 * taps, taps), f32),
            pltpu.VMEM((cb, length), bf16),
            pltpu.VMEM((cb, length), bf16),
            pltpu.VMEM((width, 2 * taps), bf16),
            pltpu.VMEM((width, 2 * taps), bf16),
            pltpu.VMEM((2 * taps, 2 * taps), bf16),
            pltpu.VMEM((taps, 3 * taps), bf16),
            pltpu.VMEM((capacity, cb_count * tiles, taps, 128), f32),
            pltpu.VMEM((length, 128), f32),
            pltpu.VMEM((cb_count * tiles, queries, 128), f32),
            pltpu.VMEM((capacity, queries, 8, 128), f32),
            pltpu.VMEM((capacity, 8, 128), f32),
            pltpu.SMEM(counts.shape, jnp.int32),
            pltpu.SMEM((queries,), jnp.int32),
            pltpu.SMEM((queries,), jnp.int32),
            pltpu.SemaphoreType.DMA((7 + cb_count,)),
            pltpu.SemaphoreType.DMA((2, capacity, cb_count)),
        ],
        compiler_params=pltpu.CompilerParams(vmem_limit_bytes=62 * 1024 * 1024),
        cost_estimate=pl.CostEstimate(flops=4 * 10**9, bytes_accessed=11 * 2**20, transcendentals=0),
    )(
        counts, query_pos, inputs, cotangent, basis, eigvals, query_context, query_cotangent,
        jnp.asarray(forward), jnp.asarray(inverse),
    )


def sum_over(value, axis):
    size = lax.axis_size(axis)
    mask = 1
    while mask < size:
        value = value + lax.ppermute(value, axis, [(i, i ^ mask) for i in range(size)])
        mask *= 2
    return value


def body(counts, inputs, cotangent, basis, eigvals, query_context, query_cotangent, query_pos):
    capacity = inputs.shape[0]
    queries = query_pos.shape[0]
    sums = local_sums(counts, inputs, cotangent, basis, eigvals, query_context, query_cotangent, query_pos)
    sums = sum_over(sums, "chan")
    return sums[:, :queries] / jnp.sqrt(sums[:, queries:])


def solution(mesh):
    return jax.shard_map(
        body,
        mesh=mesh,
        in_specs=(
            P("groups"),
            P(("groups", "dp"), None, "chan"),
            P(("groups", "dp"), None, "chan"),
            P(),
            P("chan", None),
            P(None, "chan"),
            P(None, "chan"),
            P(),
        ),
        out_specs=P(("groups", "dp"), None),
        check_vma=False,
    )
```

```python
import functools

import jax
import jax.numpy as jnp
import ml_dtypes
import numpy as np
from jax import lax
from jax.experimental import pallas as pl
from jax.experimental.pallas import tpu as pltpu
from jax.sharding import PartitionSpec as P

damping = 0.1
f32 = jnp.float32
bf16 = jnp.bfloat16


def transform_tables(taps):
    freq = np.arange(taps)
    angle = np.pi / taps * np.arange(taps)[:, None] * (freq + 0.5)[None, :]
    sign = np.where(freq % 2 == 0, 1.0, -1.0)
    real, imag = np.cos(angle), -np.sin(angle)
    forward = []
    for table in (np.concatenate([real, imag], 1), np.concatenate([sign * imag, -sign * real], 1)):
        high = table.astype(ml_dtypes.bfloat16)
        low = (table - high.astype(np.float64)).astype(ml_dtypes.bfloat16)
        forward.append(np.concatenate([high, low], 0))
    inverse = np.concatenate([np.sin(angle) * sign, np.cos(angle) * sign], 1).T / taps
    return np.stack(forward), inverse.astype(np.float32)


def split(value):
    high = value.astype(bf16)
    return high, (value - high.astype(f32)).astype(bf16)


def dot(a, b):
    return jnp.dot(a, b, preferred_element_type=f32)


def dot_nt(a, b):
    return lax.dot_general(a, b, (((1,), (1,)), ((), ())), preferred_element_type=f32)


def local_kernel(
    counts_hbm, pos_hbm, x_hbm, g_hbm, basis_hbm, eig_hbm, ctx_hbm, qct_hbm, fwd_hbm, inv_hbm, out_ref,
    xbuf, gbuf, ctxbuf, eigbuf, basisbuf, qctbuf, fwd, inv,
    x_turned, g_turned, acc_hi, acc_lo, rot_mat, back, vbuf, ctxf, ctxg, qctf, raw, norm, counts_ref, pos_ref, start_ref, sems, wsems,
):
    capacity, cb_count, length, cb = xbuf.shape
    taps = basisbuf.shape[0]
    queries = pos_ref.shape[0]
    blocks = length // taps
    tiles = cb // 128
    width = cb_count * cb

    def columns(c):
        return pl.ds(pl.multiple_of(c * cb, cb), cb)

    scalars = [
        pltpu.make_async_copy(counts_hbm, counts_ref, sems.at[5 + cb_count]),
        pltpu.make_async_copy(pos_hbm, pos_ref, sems.at[6 + cb_count]),
    ]
    small = [
        pltpu.make_async_copy(fwd_hbm, fwd, sems.at[0]),
        pltpu.make_async_copy(basis_hbm, basisbuf, sems.at[1]),
        pltpu.make_async_copy(inv_hbm, inv, sems.at[2]),
        pltpu.make_async_copy(qct_hbm, qctbuf, sems.at[3]),
        pltpu.make_async_copy(eig_hbm, eigbuf, sems.at[4]),
    ]

    def context_copy(c):
        return pltpu.make_async_copy(ctx_hbm.at[:, columns(c)], ctxbuf.at[c], sems.at[5 + c])

    def window_copies(s, c):
        return (
            pltpu.make_async_copy(x_hbm.at[s, :, columns(c)], xbuf.at[s, c], wsems.at[0, s, c]),
            pltpu.make_async_copy(g_hbm.at[s, :, columns(c)], gbuf.at[s, c], wsems.at[1, s, c]),
        )

    for copy in scalars + small[:3]:
        copy.start()
    for c in range(cb_count):
        for copy in window_copies(0, c):
            copy.start()
        if c == 0:
            for copy in small[3:]:
                copy.start()
        context_copy(c).start()
    scalars[0].wait()
    count = counts_ref[lax.axis_index("dp")]
    for s in range(1, capacity):
        @pl.when(s < count)
        def _():
            for c in range(cb_count):
                for copy in window_copies(s, c):
                    copy.start()

    raw[...] = jnp.zeros_like(raw)
    norm[...] = jnp.zeros_like(norm)
    scalars[1].wait()

    def starts(q, unused):
        start_ref[q] = jnp.clip(pos_ref[q] - (taps - 1), 0, length - taps)
        return unused

    lax.fori_loop(0, queries, starts, 0)
    for copy in small[:3]:
        copy.wait()

    base_hi, base_lo = split(basisbuf[...])
    inv_hi, inv_lo = split(inv[...])
    rot_hi, rot_lo = split(dot(inv_hi, base_hi) + (dot(inv_hi, base_lo) + dot(inv_lo, base_hi)))
    rot_mat[...] = jnp.concatenate([rot_hi, rot_lo], 1)
    row = lax.broadcasted_iota(jnp.int32, (taps, taps), 0)
    col = lax.broadcasted_iota(jnp.int32, (taps, taps), 1)
    flip = (row + col == taps - 1).astype(bf16)
    flip_hi = dot(flip, base_hi).astype(bf16)
    back[...] = jnp.concatenate([flip_hi, flip_hi, dot(flip, base_lo).astype(bf16)], 1)

    rows = 64

    def cross(first):
        def stack(parity):
            parts = []
            for b in range(blocks):
                turned = x_turned if b % 2 == parity else g_turned
                parts.append(turned[first:first + rows, b * taps:(b + 1) * taps])
            both = jnp.concatenate(parts, 0)
            return jnp.concatenate([both, both], 1)

        spectra = [dot(stack(0), fwd[0]), dot(stack(1), fwd[1])]

        def parts_of(array, b):
            block = spectra[b % 2 if array == 0 else 1 - b % 2][b * rows:(b + 1) * rows]
            return block[:, :taps], block[:, taps:]

        for b in range(blocks):
            x_re, x_im = parts_of(0, b)
            g_re, g_im = parts_of(1, b)
            if b == 0:
                t_re, t_im = -x_re, -x_im
            elif b % 2:
                t_re, t_im = prev_re + x_re, prev_im + x_im
            else:
                t_re, t_im = prev_re - x_re, prev_im - x_im
            add_re = g_re * t_re + g_im * t_im
            add_im = g_im * t_re - g_re * t_im
            sum_re = add_re if b == 0 else sum_re + add_re
            sum_im = add_im if b == 0 else sum_im + add_im
            prev_re, prev_im = x_re, x_im
        return jnp.concatenate([sum_re, sum_im], 1)

    def spectra(s, c):
        for copy in window_copies(s, c):
            copy.wait()
        for t in range(0, cb, 128):
            for turned, buf in ((x_turned, xbuf), (g_turned, gbuf)):
                turned[t:t + 128, :] = buf[s, c, :, t:t + 128].T
        for first in range(0, cb, rows):
            place = pl.ds(pl.multiple_of(c * cb + first, rows), rows)
            acc_hi[s, place, :], acc_lo[s, place, :] = split(cross(first))

    def filters(windows):
        inverse_weight = 1.0 / (eigbuf[...] + damping)
        for s in range(windows):
            twice = dot(acc_hi[s], rot_mat[...])
            rotated = twice[:, :taps] + (twice[:, taps:] + dot(acc_lo[s], rot_mat[:, :taps]))
            scaled = rotated * inverse_weight
            norm[s] = jnp.sum((scaled * rotated).reshape(width // 8, 8, taps), 0)
            high, low = split(scaled)
            turned = dot_nt(back[:, :2 * taps], jnp.concatenate([high, low], 1)) + dot_nt(back[:, 2 * taps:], high)
            for t in range(width // 128):
                vbuf[s, t] = turned[:, t * 128:(t + 1) * 128]

    def window_step(s, unused):
        def block_step(c, unused):
            spectra(s, c)
            return unused

        lax.fori_loop(0, cb_count, block_step, 0)
        return unused

    lax.fori_loop(0, count, window_step, 0)
    for c in range(cb_count):
        context_copy(c).wait()
    small[3].wait()
    for t in range(cb_count * tiles):
        qctf[t] = qctbuf[:, t * 128:(t + 1) * 128].astype(f32)

    small[4].wait()

    @pl.when(count == 0)
    def _():
        for c in range(cb_count):
            for copy in window_copies(0, c):
                copy.wait()

    halves = 2
    depth = taps // halves

    def probes(windows):
        def convert(t):
            lanes = pl.ds(pl.multiple_of(t % tiles * 128, 128), 128)
            return ctxbuf[t // tiles, :, lanes].astype(f32)

        def meet(t, buf):
            for h in range(halves):
                filt = [vbuf[s, t, h * depth:(h + 1) * depth, :] for s in range(windows)]
                for q in range(queries):
                    piece = buf[pl.ds(start_ref[q] + h * depth, depth), :]
                    cotangent = qctf[t, q:q + 1, :]
                    for s in range(windows):
                        part = jnp.sum((piece * filt[s]).reshape(depth // 8, 8, 128), 0)
                        raw[s, q] += part * cotangent

        total = width // 128
        ctxf[...] = convert(0)

        def pair_step(i, unused):
            ctxg[...] = convert(2 * i + 1)
            meet(2 * i, ctxf)
            ctxf[...] = convert(jnp.minimum(2 * i + 2, total - 1))
            meet(2 * i + 1, ctxg)
            return unused

        lax.fori_loop(0, total // 2, pair_step, 0)
        if total % 2:
            meet(total - 1, ctxf)

    for windows in range(1, capacity + 1):
        @pl.when(count == windows)
        def _():
            filters(windows)
            probes(windows)

    for s in range(capacity):
        per_query = jnp.sum(raw[s], 1)
        lane_one = (lax.broadcasted_iota(jnp.int32, (1, 128), 1) == 0).astype(f32)
        own = jnp.where(s < count, jnp.sum(norm[s], 0, keepdims=True), lane_one)
        table = jnp.concatenate([per_query, jnp.broadcast_to(own, (queries, 128))], 0)
        out_ref[pl.ds(s, 1), :] = jnp.sum(table.T, 0, keepdims=True)


def local_sums(counts, inputs, cotangent, basis, eigvals, query_context, query_cotangent, query_pos):
    capacity, length, width = inputs.shape
    taps = basis.shape[0]
    queries = query_pos.shape[0]
    cb = min(512, width)
    cb_count, tiles = width // cb, cb // 128
    forward, inverse = transform_tables(taps)
    hbm = pl.BlockSpec(memory_space=pl.ANY)
    return pl.pallas_call(
        local_kernel,
        out_shape=jax.ShapeDtypeStruct((capacity, 128), f32),
        in_specs=[hbm] * 10,
        out_specs=pl.BlockSpec(memory_space=pltpu.VMEM),
        scratch_shapes=[
            pltpu.VMEM((capacity, cb_count, length, cb), bf16),
            pltpu.VMEM((capacity, cb_count, length, cb), bf16),
            pltpu.VMEM((cb_count, length, cb), bf16),
            pltpu.VMEM((width, taps), f32),
            pltpu.VMEM((taps, taps), f32),
            pltpu.VMEM((queries, width), bf16),
            pltpu.VMEM((2, 2 * taps, 2 * taps), bf16),
            pltpu.VMEM((2 * taps, taps), f32),
            pltpu.VMEM((cb, length), bf16),
            pltpu.VMEM((cb, length), bf16),
            pltpu.VMEM((capacity, width, 2 * taps), bf16),
            pltpu.VMEM((capacity, width, 2 * taps), bf16),
            pltpu.VMEM((2 * taps, 2 * taps), bf16),
            pltpu.VMEM((taps, 3 * taps), bf16),
            pltpu.VMEM((capacity, cb_count * tiles, taps, 128), f32),
            pltpu.VMEM((length, 128), f32),
            pltpu.VMEM((length, 128), f32),
            pltpu.VMEM((cb_count * tiles, queries, 128), f32),
            pltpu.VMEM((capacity, queries, 8, 128), f32),
            pltpu.VMEM((capacity, 8, 128), f32),
            pltpu.SMEM(counts.shape, jnp.int32),
            pltpu.SMEM((queries,), jnp.int32),
            pltpu.SMEM((queries,), jnp.int32),
            pltpu.SemaphoreType.DMA((7 + cb_count,)),
            pltpu.SemaphoreType.DMA((2, capacity, cb_count)),
        ],
        compiler_params=pltpu.CompilerParams(vmem_limit_bytes=62 * 1024 * 1024),
        cost_estimate=pl.CostEstimate(flops=4 * 10**9, bytes_accessed=11 * 2**20, transcendentals=0),
    )(
        counts, query_pos, inputs, cotangent, basis, eigvals, query_context, query_cotangent,
        jnp.asarray(forward), jnp.asarray(inverse),
    )


def sum_over(value, axis):
    size = lax.axis_size(axis)
    mask = 1
    while mask < size:
        value = value + lax.ppermute(value, axis, [(i, i ^ mask) for i in range(size)])
        mask *= 2
    return value


def body(counts, inputs, cotangent, basis, eigvals, query_context, query_cotangent, query_pos):
    capacity = inputs.shape[0]
    queries = query_pos.shape[0]
    sums = local_sums(counts, inputs, cotangent, basis, eigvals, query_context, query_cotangent, query_pos)
    sums = sum_over(sums, "chan")
    return sums[:, :queries] / jnp.sqrt(sums[:, queries:])


def solution(mesh):
    return jax.shard_map(
        body,
        mesh=mesh,
        in_specs=(
            P("groups"),
            P(("groups", "dp"), None, "chan"),
            P(("groups", "dp"), None, "chan"),
            P(),
            P("chan", None),
            P(None, "chan"),
            P(None, "chan"),
            P(),
        ),
        out_specs=P(("groups", "dp"), None),
        check_vma=False,
    )
```

```python
import functools

import jax
import jax.numpy as jnp
import ml_dtypes
import numpy as np
from jax import lax
from jax.experimental import pallas as pl
from jax.experimental.pallas import tpu as pltpu
from jax.sharding import PartitionSpec as P

damping = 0.1
f32 = jnp.float32
bf16 = jnp.bfloat16


def transform_tables(taps):
    freq = np.arange(taps)
    angle = np.pi / taps * np.arange(taps)[:, None] * (freq + 0.5)[None, :]
    sign = np.where(freq % 2 == 0, 1.0, -1.0)
    real, imag = np.cos(angle), -np.sin(angle)
    forward = []
    for table in (np.concatenate([real, imag], 1), np.concatenate([sign * imag, -sign * real], 1)):
        high = table.astype(ml_dtypes.bfloat16)
        low = (table - high.astype(np.float64)).astype(ml_dtypes.bfloat16)
        forward.append(np.concatenate([high, low], 0))
    inverse = np.concatenate([np.sin(angle) * sign, np.cos(angle) * sign], 1).T / taps
    return np.stack(forward), inverse.astype(np.float32)


def split(value):
    high = value.astype(bf16)
    return high, (value - high.astype(f32)).astype(bf16)


def dot(a, b):
    return jnp.dot(a, b, preferred_element_type=f32)


def dot_nt(a, b):
    return lax.dot_general(a, b, (((1,), (1,)), ((), ())), preferred_element_type=f32)


def local_kernel(
    counts_hbm, pos_hbm, x_hbm, g_hbm, basis_hbm, eig_hbm, ctx_hbm, qct_hbm, fwd_hbm, inv_hbm, out_ref,
    xbuf, gbuf, ctxbuf, eigbuf, basisbuf, qctbuf, fwd, inv,
    x_turned, g_turned, acc_hi, acc_lo, rot_mat, back, vbuf, ctxf, ctxg, qctf, raw, norm, counts_ref, pos_ref, start_ref, sems, wsems,
):
    capacity, cb_count, length, cb = xbuf.shape
    taps = basisbuf.shape[0]
    queries = pos_ref.shape[0]
    blocks = length // taps
    tiles = cb // 128
    width = cb_count * cb

    def columns(c):
        return pl.ds(pl.multiple_of(c * cb, cb), cb)

    scalars = [
        pltpu.make_async_copy(counts_hbm, counts_ref, sems.at[5 + cb_count]),
        pltpu.make_async_copy(pos_hbm, pos_ref, sems.at[6 + cb_count]),
    ]
    small = [
        pltpu.make_async_copy(fwd_hbm, fwd, sems.at[0]),
        pltpu.make_async_copy(basis_hbm, basisbuf, sems.at[1]),
        pltpu.make_async_copy(inv_hbm, inv, sems.at[2]),
        pltpu.make_async_copy(qct_hbm, qctbuf, sems.at[3]),
        pltpu.make_async_copy(eig_hbm, eigbuf, sems.at[4]),
    ]

    def context_copy(c):
        return pltpu.make_async_copy(ctx_hbm.at[:, columns(c)], ctxbuf.at[c], sems.at[5 + c])

    def window_copies(s, c):
        return (
            pltpu.make_async_copy(x_hbm.at[s, :, columns(c)], xbuf.at[s, c], wsems.at[0, s, c]),
            pltpu.make_async_copy(g_hbm.at[s, :, columns(c)], gbuf.at[s, c], wsems.at[1, s, c]),
        )

    for copy in scalars + small[:3]:
        copy.start()
    for c in range(cb_count):
        for copy in window_copies(0, c):
            copy.start()
        if c == 0:
            for copy in small[3:]:
                copy.start()
        context_copy(c).start()
    scalars[0].wait()
    count = counts_ref[lax.axis_index("dp")]
    for s in range(1, capacity):
        @pl.when(s < count)
        def _():
            for c in range(cb_count):
                for copy in window_copies(s, c):
                    copy.start()

    raw[...] = jnp.zeros_like(raw)
    norm[...] = jnp.zeros_like(norm)
    scalars[1].wait()

    def starts(q, unused):
        start_ref[q] = jnp.clip(pos_ref[q] - (taps - 1), 0, length - taps)
        return unused

    lax.fori_loop(0, queries, starts, 0)
    for copy in small[:3]:
        copy.wait()

    base_hi, base_lo = split(basisbuf[...])
    inv_hi, inv_lo = split(inv[...])
    rot_hi, rot_lo = split(dot(inv_hi, base_hi) + (dot(inv_hi, base_lo) + dot(inv_lo, base_hi)))
    rot_mat[...] = jnp.concatenate([rot_hi, rot_lo], 1)
    row = lax.broadcasted_iota(jnp.int32, (taps, taps), 0)
    col = lax.broadcasted_iota(jnp.int32, (taps, taps), 1)
    flip = (row + col == taps - 1).astype(bf16)
    flip_hi = dot(flip, base_hi).astype(bf16)
    back[...] = jnp.concatenate([flip_hi, flip_hi, dot(flip, base_lo).astype(bf16)], 1)

    rows = 64

    def cross(first):
        def stack(parity):
            parts = []
            for b in range(blocks):
                turned = x_turned if b % 2 == parity else g_turned
                parts.append(turned[first:first + rows, b * taps:(b + 1) * taps])
            both = jnp.concatenate(parts, 0)
            return jnp.concatenate([both, both], 1)

        spectra = [dot(stack(0), fwd[0]), dot(stack(1), fwd[1])]

        def parts_of(array, b):
            block = spectra[b % 2 if array == 0 else 1 - b % 2][b * rows:(b + 1) * rows]
            return block[:, :taps], block[:, taps:]

        for b in range(blocks):
            x_re, x_im = parts_of(0, b)
            g_re, g_im = parts_of(1, b)
            if b == 0:
                t_re, t_im = -x_re, -x_im
            elif b % 2:
                t_re, t_im = prev_re + x_re, prev_im + x_im
            else:
                t_re, t_im = prev_re - x_re, prev_im - x_im
            add_re = g_re * t_re + g_im * t_im
            add_im = g_im * t_re - g_re * t_im
            sum_re = add_re if b == 0 else sum_re + add_re
            sum_im = add_im if b == 0 else sum_im + add_im
            prev_re, prev_im = x_re, x_im
        return jnp.concatenate([sum_re, sum_im], 1)

    def spectra(s, c):
        for copy in window_copies(s, c):
            copy.wait()
        for t in range(0, cb, 128):
            for turned, buf in ((x_turned, xbuf), (g_turned, gbuf)):
                turned[t:t + 128, :] = buf[s, c, :, t:t + 128].T
        for first in range(0, cb, rows):
            place = pl.ds(pl.multiple_of(c * cb + first, rows), rows)
            acc_hi[s, place, :], acc_lo[s, place, :] = split(cross(first))

    def filters(windows):
        inverse_weight = 1.0 / (eigbuf[...] + damping)
        for s in range(windows):
            twice = dot(acc_hi[s], rot_mat[...])
            rotated = twice[:, :taps] + (twice[:, taps:] + dot(acc_lo[s], rot_mat[:, :taps]))
            scaled = rotated * inverse_weight
            norm[s] = jnp.sum((scaled * rotated).reshape(width // 8, 8, taps), 0)
            high, low = split(scaled)
            turned = dot_nt(back[:, :2 * taps], jnp.concatenate([high, low], 1)) + dot_nt(back[:, 2 * taps:], high)
            for t in range(width // 128):
                vbuf[s, t] = turned[:, t * 128:(t + 1) * 128]

    def window_step(s, unused):
        def block_step(c, unused):
            spectra(s, c)
            return unused

        lax.fori_loop(0, cb_count, block_step, 0)
        return unused

    lax.fori_loop(0, count, window_step, 0)
    for c in range(cb_count):
        context_copy(c).wait()
    small[3].wait()
    for t in range(cb_count * tiles):
        qctf[t] = qctbuf[:, t * 128:(t + 1) * 128].astype(f32)

    small[4].wait()

    @pl.when(count == 0)
    def _():
        for c in range(cb_count):
            for copy in window_copies(0, c):
                copy.wait()

    halves = 2
    depth = taps // halves

    def probes(windows):
        def convert(t):
            lanes = pl.ds(pl.multiple_of(t % tiles * 128, 128), 128)
            return ctxbuf[t // tiles, :, lanes].astype(f32)

        def meet(t, buf):
            for h in range(halves):
                filt = [vbuf[s, t, h * depth:(h + 1) * depth, :] for s in range(windows)]
                for q in range(queries):
                    piece = buf[pl.ds(start_ref[q] + h * depth, depth), :]
                    cotangent = qctf[t, q:q + 1, :]
                    for s in range(windows):
                        part = jnp.sum((piece * filt[s]).reshape(depth // 8, 8, 128), 0)
                        raw[s, q] += part * cotangent

        total = width // 128
        ctxf[...] = convert(0)

        def pair_step(i, unused):
            ctxg[...] = convert(2 * i + 1)
            meet(2 * i, ctxf)
            ctxf[...] = convert(jnp.minimum(2 * i + 2, total - 1))
            meet(2 * i + 1, ctxg)
            return unused

        lax.fori_loop(0, total // 2, pair_step, 0)
        if total % 2:
            meet(total - 1, ctxf)

    for windows in range(1, capacity + 1):
        @pl.when(count == windows)
        def _():
            filters(windows)
            probes(windows)

    for s in range(capacity):
        per_query = jnp.sum(raw[s], 1)
        lane_one = (lax.broadcasted_iota(jnp.int32, (1, 128), 1) == 0).astype(f32)
        own = jnp.where(s < count, jnp.sum(norm[s], 0, keepdims=True), lane_one)
        table = jnp.concatenate([per_query, jnp.broadcast_to(own, (queries, 128))], 0)
        out_ref[pl.ds(s, 1), :] = jnp.sum(table.T, 0, keepdims=True)


def local_sums(counts, inputs, cotangent, basis, eigvals, query_context, query_cotangent, query_pos):
    capacity, length, width = inputs.shape
    taps = basis.shape[0]
    queries = query_pos.shape[0]
    cb = min(512, width)
    cb_count, tiles = width // cb, cb // 128
    forward, inverse = transform_tables(taps)
    hbm = pl.BlockSpec(memory_space=pl.ANY)
    return pl.pallas_call(
        local_kernel,
        out_shape=jax.ShapeDtypeStruct((capacity, 128), f32),
        in_specs=[hbm] * 10,
        out_specs=pl.BlockSpec(memory_space=pltpu.VMEM),
        scratch_shapes=[
            pltpu.VMEM((capacity, cb_count, length, cb), bf16),
            pltpu.VMEM((capacity, cb_count, length, cb), bf16),
            pltpu.VMEM((cb_count, length, cb), bf16),
            pltpu.VMEM((width, taps), f32),
            pltpu.VMEM((taps, taps), f32),
            pltpu.VMEM((queries, width), bf16),
            pltpu.VMEM((2, 2 * taps, 2 * taps), bf16),
            pltpu.VMEM((2 * taps, taps), f32),
            pltpu.VMEM((cb, length), bf16),
            pltpu.VMEM((cb, length), bf16),
            pltpu.VMEM((capacity, width, 2 * taps), bf16),
            pltpu.VMEM((capacity, width, 2 * taps), bf16),
            pltpu.VMEM((2 * taps, 2 * taps), bf16),
            pltpu.VMEM((taps, 3 * taps), bf16),
            pltpu.VMEM((capacity, cb_count * tiles, taps, 128), f32),
            pltpu.VMEM((length, 128), f32),
            pltpu.VMEM((length, 128), f32),
            pltpu.VMEM((cb_count * tiles, queries, 128), f32),
            pltpu.VMEM((capacity, queries, 8, 128), f32),
            pltpu.VMEM((capacity, 8, 128), f32),
            pltpu.SMEM(counts.shape, jnp.int32),
            pltpu.SMEM((queries,), jnp.int32),
            pltpu.SMEM((queries,), jnp.int32),
            pltpu.SemaphoreType.DMA((7 + cb_count,)),
            pltpu.SemaphoreType.DMA((2, capacity, cb_count)),
        ],
        compiler_params=pltpu.CompilerParams(vmem_limit_bytes=62 * 1024 * 1024),
        cost_estimate=pl.CostEstimate(flops=4 * 10**9, bytes_accessed=11 * 2**20, transcendentals=0),
    )(
        counts, query_pos, inputs, cotangent, basis, eigvals, query_context, query_cotangent,
        jnp.asarray(forward), jnp.asarray(inverse),
    )


def sum_over(sent, value, axis):
    size = lax.axis_size(axis)
    mask = 1
    while mask < size:
        value = value + lax.ppermute(sent, axis, [(i, i ^ mask) for i in range(size)])
        sent = value
        mask *= 2
    return value


def body(counts, inputs, cotangent, basis, eigvals, query_context, query_cotangent, query_pos):
    capacity = inputs.shape[0]
    queries = query_pos.shape[0]
    sums = local_sums(counts, inputs, cotangent, basis, eigvals, query_context, query_cotangent, query_pos)
    lane = lax.broadcasted_iota(jnp.int32, sums.shape, 1)
    again = lax.optimization_barrier(jnp.where(lane < queries, sums, jnp.abs(sums)))
    sums = sum_over(sums, again, "chan")
    return sums[:, :queries] / jnp.sqrt(sums[:, queries:])


def solution(mesh):
    return jax.shard_map(
        body,
        mesh=mesh,
        in_specs=(
            P("groups"),
            P(("groups", "dp"), None, "chan"),
            P(("groups", "dp"), None, "chan"),
            P(),
            P("chan", None),
            P(None, "chan"),
            P(None, "chan"),
            P(),
        ),
        out_specs=P(("groups", "dp"), None),
        check_vma=False,
    )
```

```python
import functools

import jax
import jax.numpy as jnp
import ml_dtypes
import numpy as np
from jax import lax
from jax.experimental import pallas as pl
from jax.experimental.pallas import tpu as pltpu
from jax.sharding import PartitionSpec as P

damping = 0.1
f32 = jnp.float32
bf16 = jnp.bfloat16


def transform_tables(taps):
    freq = np.arange(taps)
    angle = np.pi / taps * np.arange(taps)[:, None] * (freq + 0.5)[None, :]
    sign = np.where(freq % 2 == 0, 1.0, -1.0)
    real, imag = np.cos(angle), -np.sin(angle)
    forward = []
    for table in (np.concatenate([real, imag], 1), np.concatenate([sign * imag, -sign * real], 1)):
        high = table.astype(ml_dtypes.bfloat16)
        low = (table - high.astype(np.float64)).astype(ml_dtypes.bfloat16)
        forward.append(np.concatenate([high, low], 0))
    inverse = np.concatenate([np.sin(angle) * sign, np.cos(angle) * sign], 1).T / taps
    return np.stack(forward), inverse.astype(np.float32)


def split(value):
    high = value.astype(bf16)
    return high, (value - high.astype(f32)).astype(bf16)


def dot(a, b):
    return jnp.dot(a, b, preferred_element_type=f32)


def dot_nt(a, b):
    return lax.dot_general(a, b, (((1,), (1,)), ((), ())), preferred_element_type=f32)


def local_kernel(
    counts_hbm, pos_hbm, x_hbm, g_hbm, basis_hbm, eig_hbm, ctx_hbm, qct_hbm, fwd_hbm, inv_hbm, out_ref,
    xbuf, gbuf, ctxbuf, eigbuf, basisbuf, qctbuf, fwd, inv,
    x_turned, g_turned, acc_hi, acc_lo, rot_mat, back, vbuf, ctxf, ctxg, qctf, raw, held, norm, counts_ref, pos_ref, start_ref, sems, wsems,
):
    capacity, cb_count, length, cb = xbuf.shape
    taps = basisbuf.shape[0]
    queries = pos_ref.shape[0]
    blocks = length // taps
    tiles = cb // 128
    width = cb_count * cb

    def columns(c):
        return pl.ds(pl.multiple_of(c * cb, cb), cb)

    scalars = [
        pltpu.make_async_copy(counts_hbm, counts_ref, sems.at[5 + cb_count]),
        pltpu.make_async_copy(pos_hbm, pos_ref, sems.at[6 + cb_count]),
    ]
    small = [
        pltpu.make_async_copy(fwd_hbm, fwd, sems.at[0]),
        pltpu.make_async_copy(basis_hbm, basisbuf, sems.at[1]),
        pltpu.make_async_copy(inv_hbm, inv, sems.at[2]),
        pltpu.make_async_copy(qct_hbm, qctbuf, sems.at[3]),
        pltpu.make_async_copy(eig_hbm, eigbuf, sems.at[4]),
    ]

    def context_copy(c):
        return pltpu.make_async_copy(ctx_hbm.at[:, columns(c)], ctxbuf.at[c], sems.at[5 + c])

    def window_copies(s, c):
        return (
            pltpu.make_async_copy(x_hbm.at[s, :, columns(c)], xbuf.at[s, c], wsems.at[0, s, c]),
            pltpu.make_async_copy(g_hbm.at[s, :, columns(c)], gbuf.at[s, c], wsems.at[1, s, c]),
        )

    for copy in scalars + small[:3]:
        copy.start()
    for c in range(cb_count):
        for copy in window_copies(0, c):
            copy.start()
        if c == 0:
            for copy in small[3:]:
                copy.start()
        context_copy(c).start()
    scalars[0].wait()
    count = counts_ref[lax.axis_index("dp")]
    for s in range(1, capacity):
        @pl.when(s < count)
        def _():
            for c in range(cb_count):
                for copy in window_copies(s, c):
                    copy.start()

    raw[...] = jnp.zeros_like(raw)
    norm[...] = jnp.zeros_like(norm)
    scalars[1].wait()

    def starts(q, unused):
        start_ref[q] = jnp.clip(pos_ref[q] - (taps - 1), 0, length - taps)
        return unused

    lax.fori_loop(0, queries, starts, 0)
    for copy in small[:3]:
        copy.wait()

    base_hi, base_lo = split(basisbuf[...])
    inv_hi, inv_lo = split(inv[...])
    rot_hi, rot_lo = split(dot(inv_hi, base_hi) + (dot(inv_hi, base_lo) + dot(inv_lo, base_hi)))
    rot_mat[...] = jnp.concatenate([rot_hi, rot_lo], 1)
    row = lax.broadcasted_iota(jnp.int32, (taps, taps), 0)
    col = lax.broadcasted_iota(jnp.int32, (taps, taps), 1)
    flip = (row + col == taps - 1).astype(bf16)
    flip_hi = dot(flip, base_hi).astype(bf16)
    back[...] = jnp.concatenate([flip_hi, flip_hi, dot(flip, base_lo).astype(bf16)], 1)

    rows = 64

    def cross(first):
        def stack(parity):
            parts = []
            for b in range(blocks):
                turned = x_turned if b % 2 == parity else g_turned
                parts.append(turned[first:first + rows, b * taps:(b + 1) * taps])
            both = jnp.concatenate(parts, 0)
            return jnp.concatenate([both, both], 1)

        spectra = [dot(stack(0), fwd[0]), dot(stack(1), fwd[1])]

        def parts_of(array, b):
            block = spectra[b % 2 if array == 0 else 1 - b % 2][b * rows:(b + 1) * rows]
            return block[:, :taps], block[:, taps:]

        for b in range(blocks):
            x_re, x_im = parts_of(0, b)
            g_re, g_im = parts_of(1, b)
            if b == 0:
                t_re, t_im = -x_re, -x_im
            elif b % 2:
                t_re, t_im = prev_re + x_re, prev_im + x_im
            else:
                t_re, t_im = prev_re - x_re, prev_im - x_im
            add_re = g_re * t_re + g_im * t_im
            add_im = g_im * t_re - g_re * t_im
            sum_re = add_re if b == 0 else sum_re + add_re
            sum_im = add_im if b == 0 else sum_im + add_im
            prev_re, prev_im = x_re, x_im
        return jnp.concatenate([sum_re, sum_im], 1)

    def spectra(s, c):
        for copy in window_copies(s, c):
            copy.wait()
        for t in range(0, cb, 128):
            for turned, buf in ((x_turned, xbuf), (g_turned, gbuf)):
                turned[t:t + 128, :] = buf[s, c, :, t:t + 128].T
        for first in range(0, cb, rows):
            place = pl.ds(pl.multiple_of(c * cb + first, rows), rows)
            acc_hi[s, place, :], acc_lo[s, place, :] = split(cross(first))

    def filters(windows):
        inverse_weight = 1.0 / (eigbuf[...] + damping)
        high = jnp.concatenate([acc_hi[s] for s in range(windows)], 0)
        low = jnp.concatenate([acc_lo[s] for s in range(windows)], 0)
        twice = dot(high, rot_mat[...])
        rotated = twice[:, :taps] + (twice[:, taps:] + dot(low, rot_mat[:, :taps]))
        scaled = rotated * jnp.concatenate([inverse_weight] * windows, 0)
        squares = scaled * rotated
        for s in range(windows):
            norm[s] = jnp.sum(squares[s * width:(s + 1) * width].reshape(width // 8, 8, taps), 0)
        high, low = split(scaled)
        turned = dot_nt(back[:, :2 * taps], jnp.concatenate([high, low], 1)) + dot_nt(back[:, 2 * taps:], high)
        for t in range(windows * width // 128):
            vbuf[t * 128 // width, t % (width // 128)] = turned[:, t * 128:(t + 1) * 128]

    def window_step(s, unused):
        def block_step(c, unused):
            spectra(s, c)
            return unused

        lax.fori_loop(0, cb_count, block_step, 0)
        return unused

    lax.fori_loop(0, count, window_step, 0)
    for c in range(cb_count):
        context_copy(c).wait()
    small[3].wait()
    for t in range(cb_count * tiles):
        qctf[t] = qctbuf[:, t * 128:(t + 1) * 128].astype(f32)

    small[4].wait()

    @pl.when(count == 0)
    def _():
        for c in range(cb_count):
            for copy in window_copies(0, c):
                copy.wait()

    halves = 2
    depth = taps // halves

    def probes(windows):
        def convert(t):
            lanes = pl.ds(pl.multiple_of(t % tiles * 128, 128), 128)
            return ctxbuf[t // tiles, :, lanes].astype(f32)

        def meet(t, buf):
            for h in range(halves):
                filt = [vbuf[s, t, h * depth:(h + 1) * depth, :] for s in range(windows)]
                for q in range(queries):
                    piece = buf[pl.ds(start_ref[q] + h * depth, depth), :]
                    for s in range(windows):
                        part = jnp.sum((piece * filt[s]).reshape(depth // 8, 8, 128), 0)
                        if h > 0:
                            part += held[s, q]
                        if h < halves - 1:
                            held[s, q] = part
                        else:
                            raw[s, q] += part * qctf[t, q:q + 1, :]

        total = width // 128
        ctxf[...] = convert(0)

        def pair_step(i, unused):
            ctxg[...] = convert(2 * i + 1)
            meet(2 * i, ctxf)
            ctxf[...] = convert(jnp.minimum(2 * i + 2, total - 1))
            meet(2 * i + 1, ctxg)
            return unused

        lax.fori_loop(0, total // 2, pair_step, 0)
        if total % 2:
            meet(total - 1, ctxf)

    for windows in range(1, capacity + 1):
        @pl.when(count == windows)
        def _():
            filters(windows)
            probes(windows)

    for s in range(capacity):
        per_query = jnp.sum(raw[s], 1)
        lane_one = (lax.broadcasted_iota(jnp.int32, (1, 128), 1) == 0).astype(f32)
        own = jnp.where(s < count, jnp.sum(norm[s], 0, keepdims=True), lane_one)
        table = jnp.concatenate([per_query, jnp.broadcast_to(own, (queries, 128))], 0)
        out_ref[pl.ds(s, 1), :] = jnp.sum(table.T, 0, keepdims=True)


def local_sums(counts, inputs, cotangent, basis, eigvals, query_context, query_cotangent, query_pos):
    capacity, length, width = inputs.shape
    taps = basis.shape[0]
    queries = query_pos.shape[0]
    cb = min(512, width)
    cb_count, tiles = width // cb, cb // 128
    forward, inverse = transform_tables(taps)
    hbm = pl.BlockSpec(memory_space=pl.ANY)
    return pl.pallas_call(
        local_kernel,
        out_shape=jax.ShapeDtypeStruct((capacity, 128), f32),
        in_specs=[hbm] * 10,
        out_specs=pl.BlockSpec(memory_space=pltpu.VMEM),
        scratch_shapes=[
            pltpu.VMEM((capacity, cb_count, length, cb), bf16),
            pltpu.VMEM((capacity, cb_count, length, cb), bf16),
            pltpu.VMEM((cb_count, length, cb), bf16),
            pltpu.VMEM((width, taps), f32),
            pltpu.VMEM((taps, taps), f32),
            pltpu.VMEM((queries, width), bf16),
            pltpu.VMEM((2, 2 * taps, 2 * taps), bf16),
            pltpu.VMEM((2 * taps, taps), f32),
            pltpu.VMEM((cb, length), bf16),
            pltpu.VMEM((cb, length), bf16),
            pltpu.VMEM((capacity, width, 2 * taps), bf16),
            pltpu.VMEM((capacity, width, 2 * taps), bf16),
            pltpu.VMEM((2 * taps, 2 * taps), bf16),
            pltpu.VMEM((taps, 3 * taps), bf16),
            pltpu.VMEM((capacity, cb_count * tiles, taps, 128), f32),
            pltpu.VMEM((length, 128), f32),
            pltpu.VMEM((length, 128), f32),
            pltpu.VMEM((cb_count * tiles, queries, 128), f32),
            pltpu.VMEM((capacity, queries, 8, 128), f32),
            pltpu.VMEM((capacity, queries, 8, 128), f32),
            pltpu.VMEM((capacity, 8, 128), f32),
            pltpu.SMEM(counts.shape, jnp.int32),
            pltpu.SMEM((queries,), jnp.int32),
            pltpu.SMEM((queries,), jnp.int32),
            pltpu.SemaphoreType.DMA((7 + cb_count,)),
            pltpu.SemaphoreType.DMA((2, capacity, cb_count)),
        ],
        compiler_params=pltpu.CompilerParams(vmem_limit_bytes=62 * 1024 * 1024),
        cost_estimate=pl.CostEstimate(flops=4 * 10**9, bytes_accessed=11 * 2**20, transcendentals=0),
    )(
        counts, query_pos, inputs, cotangent, basis, eigvals, query_context, query_cotangent,
        jnp.asarray(forward), jnp.asarray(inverse),
    )


def sum_over(sent, value, axis):
    size = lax.axis_size(axis)
    mask = 1
    while mask < size:
        value = value + lax.ppermute(sent, axis, [(i, i ^ mask) for i in range(size)])
        sent = value
        mask *= 2
    return value


def body(counts, inputs, cotangent, basis, eigvals, query_context, query_cotangent, query_pos):
    capacity = inputs.shape[0]
    queries = query_pos.shape[0]
    sums = local_sums(counts, inputs, cotangent, basis, eigvals, query_context, query_cotangent, query_pos)
    lane = lax.broadcasted_iota(jnp.int32, sums.shape, 1)
    again = lax.optimization_barrier(jnp.where(lane < queries, sums, jnp.abs(sums)))
    sums = sum_over(sums, again, "chan")
    return sums[:, :queries] / jnp.sqrt(sums[:, queries:])


def solution(mesh):
    return jax.shard_map(
        body,
        mesh=mesh,
        in_specs=(
            P("groups"),
            P(("groups", "dp"), None, "chan"),
            P(("groups", "dp"), None, "chan"),
            P(),
            P("chan", None),
            P(None, "chan"),
            P(None, "chan"),
            P(),
        ),
        out_specs=P(("groups", "dp"), None),
        check_vma=False,
    )
```

```python
import functools

import jax
import jax.numpy as jnp
import ml_dtypes
import numpy as np
from jax import lax
from jax.experimental import pallas as pl
from jax.experimental.pallas import tpu as pltpu
from jax.sharding import PartitionSpec as P

damping = 0.1
f32 = jnp.float32
bf16 = jnp.bfloat16


def transform_tables(taps):
    freq = np.arange(taps)
    angle = np.pi / taps * np.arange(taps)[:, None] * (freq + 0.5)[None, :]
    sign = np.where(freq % 2 == 0, 1.0, -1.0)
    real, imag = np.cos(angle), -np.sin(angle)
    forward = []
    for table in (np.concatenate([real, imag], 1), np.concatenate([sign * imag, -sign * real], 1)):
        high = table.astype(ml_dtypes.bfloat16)
        low = (table - high.astype(np.float64)).astype(ml_dtypes.bfloat16)
        forward.append(np.concatenate([high, low], 0))
    inverse = np.concatenate([np.sin(angle) * sign, np.cos(angle) * sign], 1).T / taps
    return np.stack(forward), inverse.astype(np.float32)


def split(value):
    high = value.astype(bf16)
    return high, (value - high.astype(f32)).astype(bf16)


def dot(a, b):
    return jnp.dot(a, b, preferred_element_type=f32)


def dot_nt(a, b):
    return lax.dot_general(a, b, (((1,), (1,)), ((), ())), preferred_element_type=f32)


def local_kernel(
    counts_hbm, pos_hbm, x_hbm, g_hbm, basis_hbm, eig_hbm, ctx_hbm, qct_hbm, fwd_hbm, inv_hbm, out_ref,
    xbuf, gbuf, ctxbuf, eigbuf, basisbuf, qctbuf, fwd, inv,
    x_turned, g_turned, acc_hi, acc_lo, rot_mat, back, vbuf, ctxf, ctxg, qctf, raw, held, norm, counts_ref, pos_ref, start_ref, sems, wsems,
):
    capacity, cb_count, length, cb = xbuf.shape
    taps = basisbuf.shape[0]
    queries = pos_ref.shape[0]
    blocks = length // taps
    tiles = cb // 128
    width = cb_count * cb

    def columns(c):
        return pl.ds(pl.multiple_of(c * cb, cb), cb)

    scalars = [
        pltpu.make_async_copy(counts_hbm, counts_ref, sems.at[5 + cb_count]),
        pltpu.make_async_copy(pos_hbm, pos_ref, sems.at[6 + cb_count]),
    ]
    small = [
        pltpu.make_async_copy(fwd_hbm, fwd, sems.at[0]),
        pltpu.make_async_copy(basis_hbm, basisbuf, sems.at[1]),
        pltpu.make_async_copy(inv_hbm, inv, sems.at[2]),
        pltpu.make_async_copy(qct_hbm, qctbuf, sems.at[3]),
        pltpu.make_async_copy(eig_hbm, eigbuf, sems.at[4]),
    ]

    def context_copy(c):
        return pltpu.make_async_copy(ctx_hbm.at[:, columns(c)], ctxbuf.at[c], sems.at[5 + c])

    def window_copies(s, c):
        return (
            pltpu.make_async_copy(x_hbm.at[s, :, columns(c)], xbuf.at[s, c], wsems.at[0, s, c]),
            pltpu.make_async_copy(g_hbm.at[s, :, columns(c)], gbuf.at[s, c], wsems.at[1, s, c]),
        )

    for copy in scalars + small[:3]:
        copy.start()
    for c in range(cb_count):
        for copy in window_copies(0, c):
            copy.start()
        if c == 0:
            for copy in small[3:]:
                copy.start()
        context_copy(c).start()
    scalars[0].wait()
    count = counts_ref[lax.axis_index("dp")]
    for s in range(1, capacity):
        @pl.when(s < count)
        def _():
            for c in range(cb_count):
                for copy in window_copies(s, c):
                    copy.start()

    raw[...] = jnp.zeros_like(raw)
    norm[...] = jnp.zeros_like(norm)
    scalars[1].wait()

    def starts(q, unused):
        start_ref[q] = jnp.clip(pos_ref[q] - (taps - 1), 0, length - taps)
        return unused

    lax.fori_loop(0, queries, starts, 0)
    for copy in small[:3]:
        copy.wait()

    base_hi, base_lo = split(basisbuf[...])
    inv_hi, inv_lo = split(inv[...])
    rot_hi, rot_lo = split(dot(inv_hi, base_hi) + (dot(inv_hi, base_lo) + dot(inv_lo, base_hi)))
    rot_mat[...] = jnp.concatenate([rot_hi, rot_lo], 1)
    row = lax.broadcasted_iota(jnp.int32, (taps, taps), 0)
    col = lax.broadcasted_iota(jnp.int32, (taps, taps), 1)
    flip = (row + col == taps - 1).astype(bf16)
    flip_hi = dot(flip, base_hi).astype(bf16)
    back[...] = jnp.concatenate([flip_hi, flip_hi, dot(flip, base_lo).astype(bf16)], 1)

    rows = 64

    def cross(first):
        def stack(parity):
            parts = []
            for b in range(blocks):
                turned = x_turned if b % 2 == parity else g_turned
                parts.append(turned[first:first + rows, b * taps:(b + 1) * taps])
            both = jnp.concatenate(parts, 0)
            return jnp.concatenate([both, both], 1)

        spectra = [dot(stack(0), fwd[0]), dot(stack(1), fwd[1])]

        def parts_of(array, b):
            block = spectra[b % 2 if array == 0 else 1 - b % 2][b * rows:(b + 1) * rows]
            return block[:, :taps], block[:, taps:]

        for b in range(blocks):
            x_re, x_im = parts_of(0, b)
            g_re, g_im = parts_of(1, b)
            if b == 0:
                t_re, t_im = -x_re, -x_im
            elif b % 2:
                t_re, t_im = prev_re + x_re, prev_im + x_im
            else:
                t_re, t_im = prev_re - x_re, prev_im - x_im
            add_re = g_re * t_re + g_im * t_im
            add_im = g_im * t_re - g_re * t_im
            sum_re = add_re if b == 0 else sum_re + add_re
            sum_im = add_im if b == 0 else sum_im + add_im
            prev_re, prev_im = x_re, x_im
        return jnp.concatenate([sum_re, sum_im], 1)

    def spectra(s, c):
        for copy in window_copies(s, c):
            copy.wait()
        for t in range(0, cb, 128):
            for turned, buf in ((x_turned, xbuf), (g_turned, gbuf)):
                turned[t:t + 128, :] = buf[s, c, :, t:t + 128].T
        for first in range(0, cb, rows):
            place = pl.ds(pl.multiple_of(c * cb + first, rows), rows)
            acc_hi[s, place, :], acc_lo[s, place, :] = split(cross(first))

    def filters(windows):
        inverse_weight = 1.0 / (eigbuf[...] + damping)
        high = jnp.concatenate([acc_hi[s] for s in range(windows)], 0)
        low = jnp.concatenate([acc_lo[s] for s in range(windows)], 0)
        twice = dot(high, rot_mat[...])
        rotated = twice[:, :taps] + (twice[:, taps:] + dot(low, rot_mat[:, :taps]))
        scaled = rotated * jnp.concatenate([inverse_weight] * windows, 0)
        squares = scaled * rotated
        for s in range(windows):
            norm[s] = jnp.sum(squares[s * width:(s + 1) * width].reshape(width // 8, 8, taps), 0)
        high, low = split(scaled)
        turned = dot_nt(back[...], jnp.concatenate([high, low, high], 1))
        for t in range(windows * width // 128):
            vbuf[t * 128 // width, t % (width // 128)] = turned[:, t * 128:(t + 1) * 128]

    def window_step(s, unused):
        def block_step(c, unused):
            spectra(s, c)
            return unused

        lax.fori_loop(0, cb_count, block_step, 0)
        return unused

    lax.fori_loop(0, count, window_step, 0)
    for c in range(cb_count):
        context_copy(c).wait()
    small[3].wait()
    for t in range(cb_count * tiles):
        qctf[t] = qctbuf[:, t * 128:(t + 1) * 128].astype(f32)

    small[4].wait()

    @pl.when(count == 0)
    def _():
        for c in range(cb_count):
            for copy in window_copies(0, c):
                copy.wait()

    halves = 2
    depth = taps // halves

    def probes(windows):
        def convert(t):
            lanes = pl.ds(pl.multiple_of(t % tiles * 128, 128), 128)
            return ctxbuf[t // tiles, :, lanes].astype(f32)

        def meet(t, buf):
            for h in range(halves):
                filt = [vbuf[s, t, h * depth:(h + 1) * depth, :] for s in range(windows)]
                for q in range(queries):
                    piece = buf[pl.ds(start_ref[q] + h * depth, depth), :]
                    for s in range(windows):
                        part = jnp.sum((piece * filt[s]).reshape(depth // 8, 8, 128), 0)
                        if h > 0:
                            part += held[s, q]
                        if h < halves - 1:
                            held[s, q] = part
                        else:
                            raw[s, q] += part * qctf[t, q:q + 1, :]

        total = width // 128
        ctxf[...] = convert(0)

        def pair_step(i, unused):
            ctxg[...] = convert(2 * i + 1)
            meet(2 * i, ctxf)
            ctxf[...] = convert(jnp.minimum(2 * i + 2, total - 1))
            meet(2 * i + 1, ctxg)
            return unused

        lax.fori_loop(0, total // 2, pair_step, 0)
        if total % 2:
            meet(total - 1, ctxf)

    for windows in range(1, capacity + 1):
        @pl.when(count == windows)
        def _():
            filters(windows)
            probes(windows)

    for s in range(capacity):
        per_query = jnp.sum(raw[s], 1)
        lane_one = (lax.broadcasted_iota(jnp.int32, (1, 128), 1) == 0).astype(f32)
        own = jnp.where(s < count, jnp.sum(norm[s], 0, keepdims=True), lane_one)
        table = jnp.concatenate([per_query, jnp.broadcast_to(own, (queries, 128))], 0)
        out_ref[pl.ds(s, 1), :] = jnp.sum(table.T, 0, keepdims=True)


def local_sums(counts, inputs, cotangent, basis, eigvals, query_context, query_cotangent, query_pos):
    capacity, length, width = inputs.shape
    taps = basis.shape[0]
    queries = query_pos.shape[0]
    cb = min(512, width)
    cb_count, tiles = width // cb, cb // 128
    forward, inverse = transform_tables(taps)
    hbm = pl.BlockSpec(memory_space=pl.ANY)
    return pl.pallas_call(
        local_kernel,
        out_shape=jax.ShapeDtypeStruct((capacity, 128), f32),
        in_specs=[hbm] * 10,
        out_specs=pl.BlockSpec(memory_space=pltpu.VMEM),
        scratch_shapes=[
            pltpu.VMEM((capacity, cb_count, length, cb), bf16),
            pltpu.VMEM((capacity, cb_count, length, cb), bf16),
            pltpu.VMEM((cb_count, length, cb), bf16),
            pltpu.VMEM((width, taps), f32),
            pltpu.VMEM((taps, taps), f32),
            pltpu.VMEM((queries, width), bf16),
            pltpu.VMEM((2, 2 * taps, 2 * taps), bf16),
            pltpu.VMEM((2 * taps, taps), f32),
            pltpu.VMEM((cb, length), bf16),
            pltpu.VMEM((cb, length), bf16),
            pltpu.VMEM((capacity, width, 2 * taps), bf16),
            pltpu.VMEM((capacity, width, 2 * taps), bf16),
            pltpu.VMEM((2 * taps, 2 * taps), bf16),
            pltpu.VMEM((taps, 3 * taps), bf16),
            pltpu.VMEM((capacity, cb_count * tiles, taps, 128), f32),
            pltpu.VMEM((length, 128), f32),
            pltpu.VMEM((length, 128), f32),
            pltpu.VMEM((cb_count * tiles, queries, 128), f32),
            pltpu.VMEM((capacity, queries, 8, 128), f32),
            pltpu.VMEM((capacity, queries, 8, 128), f32),
            pltpu.VMEM((capacity, 8, 128), f32),
            pltpu.SMEM(counts.shape, jnp.int32),
            pltpu.SMEM((queries,), jnp.int32),
            pltpu.SMEM((queries,), jnp.int32),
            pltpu.SemaphoreType.DMA((7 + cb_count,)),
            pltpu.SemaphoreType.DMA((2, capacity, cb_count)),
        ],
        compiler_params=pltpu.CompilerParams(vmem_limit_bytes=62 * 1024 * 1024),
        cost_estimate=pl.CostEstimate(flops=4 * 10**9, bytes_accessed=11 * 2**20, transcendentals=0),
    )(
        counts, query_pos, inputs, cotangent, basis, eigvals, query_context, query_cotangent,
        jnp.asarray(forward), jnp.asarray(inverse),
    )


def sum_over(sent, value, axis):
    size = lax.axis_size(axis)
    mask = 1
    while mask < size:
        value = value + lax.ppermute(sent, axis, [(i, i ^ mask) for i in range(size)])
        sent = value
        mask *= 2
    return value


def body(counts, inputs, cotangent, basis, eigvals, query_context, query_cotangent, query_pos):
    capacity = inputs.shape[0]
    queries = query_pos.shape[0]
    sums = local_sums(counts, inputs, cotangent, basis, eigvals, query_context, query_cotangent, query_pos)
    lane = lax.broadcasted_iota(jnp.int32, sums.shape, 1)
    again = lax.optimization_barrier(jnp.where(lane < queries, sums, jnp.abs(sums)))
    sums = sum_over(sums, again, "chan")
    return sums[:, :queries] / jnp.sqrt(sums[:, queries:])


def solution(mesh):
    return jax.shard_map(
        body,
        mesh=mesh,
        in_specs=(
            P("groups"),
            P(("groups", "dp"), None, "chan"),
            P(("groups", "dp"), None, "chan"),
            P(),
            P("chan", None),
            P(None, "chan"),
            P(None, "chan"),
            P(),
        ),
        out_specs=P(("groups", "dp"), None),
        check_vma=False,
    )
```
